1024 devices in a mesh: group: 32 (over y, x, core), ep: 32 (over z).
Axes of the slice: x: 4, y: 4, z: 32, core: 2. Of those that a mesh axis runs over, the one named last changes fastest.
Arguments:
- tokens: bfloat16 [131072, 2048], P(('group', 'ep')), may hold values from -6 to 6
- cotangent: bfloat16 [131072, 2048], P(('group', 'ep')), may hold values from -12 to 12
- gate_prob: bfloat16 [131072, 1], P(('group', 'ep')), may hold values from 0.099609375 to 1
- expert_ids: int32 [131072, 1], P(('group', 'ep')), may hold values from 0 to 31; in each aligned block of 128 rows (0 to 127, 128 to 255, ...) at most 5 rows name the same one
- gate_weight: bfloat16 [32, 2048, 512], P('ep'), may hold values from -0.125 to 0.125
- up_weight: bfloat16 [32, 2048, 512], P('ep'), may hold values from -0.125 to 0.125
- down_weight: bfloat16 [32, 2048, 512], P('ep'), may hold values from -0.25 to 0.25
Outputs:
- grad_tokens: bfloat16 [131072, 2048], P(('group', 'ep'))
- grad_prob: bfloat16 [131072, 1], P(('group', 'ep'))
- grad_gate: float32 [32, 2048, 512], P('ep', 'group')
- grad_up: float32 [32, 2048, 512], P('ep', 'group')
- grad_down: float32 [32, 2048, 512], P('ep', 'group')
The draws below stay inside these ranges and needn't reach their ends.
Inputs may be any that keep to these rules, and one draw needn't show every extreme that they name: `expert_ids`: among the 128 rows of one device no expert is named more than 5 times, a bound that some block reaches; every expert is named by some row.
All inputs are finite; a program needn't handle non-finite values.
Results may differ from the reference program's by a relative error of at most 0.018.
Values may be sent and summed in bfloat16 or wider, within the bound.
A program may use at most 64 MiB of HBM per device.

```python
import math
import jax
import jax.numpy as jnp
import numpy as np
from jax import lax

D = 2048
H = 512
TOK_DEV = 128
TOP = 1
EXPERTS = 32
CAP = 5
TOKENS = 131072


def with_spikes(result, rng, source, target, parts, factor):
    def block_of(dim):
        return (jnp.arange(result.shape[dim]) // (result.shape[dim] // parts)).reshape((-1,) + (1,) * (result.ndim - 1 - dim))

    one_side = jax.random.permutation(rng, parts)[block_of(target)]
    other_side = (block_of(target) + parts // 2) % parts
    return jnp.where((block_of(source) == one_side) | (block_of(source) == other_side), factor * result, result)


def steps_of(own_key, dims, pieces, smallest, top_value):
    def one(axis_at, blocks):
        draws = jax.random.uniform(jax.random.fold_in(jax.random.fold_in(own_key, 6), axis_at), (blocks,), jnp.float32, smallest / len(pieces), top_value / len(pieces))
        return jnp.repeat(jnp.exp(draws), dims[axis_at] // blocks).reshape((-1,) + (1,) * (len(dims) - axis_at - 1))

    loudness = one(*pieces[0])
    for cut in pieces[1:]:
        loudness = loudness * one(*cut)
    return loudness


def deal_out(rng, own, number, rows, amount, top, most, slope):
    sequence = jax.random.permutation(rng, amount)
    heavy_load, ordinary = portions_of(amount, rows * top, most, slope, True), portions_of(amount, rows * top, most, slope, False)
    places = jnp.arange(amount)

    def named(lengths, turn):
        used = int((lengths > 0).sum())
        fixed = max(1, used // 4)
        passed = fixed + (places - fixed + turn * (used - fixed)) % max(1, amount - fixed)
        return jnp.zeros((amount,), jnp.int32).at[sequence[jnp.where(places < fixed, places, passed)]].set(jnp.asarray(lengths, jnp.int32))

    lengths = jnp.where(number % 4 == 0, named(heavy_load, number // 4), named(ordinary, number - number // 4 - 1))
    mixed = jax.random.permutation(jax.random.fold_in(own, 3), amount)
    donor, receiver = mixed[0:amount // 2 * 2:2], mixed[1:amount // 2 * 2:2]
    room = jnp.minimum(lengths[donor] - 1, most - lengths[receiver]) // 2
    room = jnp.where((donor == sequence[0]) | (receiver == sequence[0]) | (lengths[receiver] == 0), 0, jnp.maximum(room, 0))
    passed = jax.random.randint(jax.random.fold_in(own, 4), (amount // 2,), 0, 1 << 20) % (room + 1)
    lengths = lengths.at[donor].add(-passed).at[receiver].add(passed)
    members = jnp.searchsorted(jnp.cumsum(lengths), jnp.arange(rows * top), side="right").astype(jnp.int32)
    table = members.reshape(top, rows).T
    table = table[jax.random.permutation(jax.random.fold_in(own, 1), rows)]
    turn = jax.random.randint(jax.random.fold_in(own, 2), (rows, 1), 0, top)
    return jnp.take_along_axis(table, (jnp.arange(top)[None, :] + turn) % top, axis=1)


def portions_of(amount, total, bound, slope, full):
    weights = [(1 << 20) // math.isqrt(standing ** slope) + 1 for standing in range(1, amount + 1)]
    largest = bound if full else min(bound, max(-(-total // amount), total * weights[0] // sum(weights)))
    least = 1 if total - largest >= amount - 1 else 0
    given, rest = [largest] + [least] * (amount - 1), total - largest - least * (amount - 1)
    while rest > 0:
        movable = [i for i in range(1, amount) if given[i] < largest] or [i for i in range(1, amount) if given[i] < bound]
        pool, left = sum([weights[i] for i in movable]), rest
        for i in movable:
            extra = min(bound - given[i], max(1, left * weights[i] // pool), rest)
            given[i] = given[i] + extra
            rest = rest - extra
    return np.array(given)


def bell_draw(rng, extent, spread, most, pieces=(), held_as=jnp.bfloat16):
    values = jax.random.normal(rng, extent, jnp.float32) * spread
    if len(pieces) > 0:
        values = steps_of(rng, extent, pieces, -0.22, 0.18) * values
    return jnp.clip(values, min=-most, max=most).astype(held_as)


def noise_with(own_key, shape, deviation, most, shards, heavy, kind=jnp.bfloat16):
    entries = deviation * jax.random.normal(own_key, shape, jnp.float32)
    if shards:
        entries = entries * steps_of(own_key, shape, shards, -0.22, 0.18)
    return jnp.clip(with_spikes(entries, jax.random.fold_in(own_key, 3), *heavy), -most, most).astype(kind)


def setup_inputs(seed: int = 0) -> dict:
    keys = jax.random.split(jax.random.key(seed), 8)
    tokens = bell_draw(keys[0], (TOKENS, D), 1.0, 6.0, ((0, 1024),))
    cotangent = noise_with(keys[1], (TOKENS, D), 0.5, 12.0, ((0, 1024),), (0, 1, 1024, 6.0))
    gate_prob = jnp.clip(0.099609375 + 0.9003906 * jax.random.uniform(keys[2], (TOKENS, TOP), jnp.float32) ** steps_of(keys[2], (TOKENS, TOP), ((0, 1024),), -0.2, 0.2), 0.099609375, 1.0).astype(jnp.bfloat16)
    expert_ids_keys = jax.random.split(jax.random.fold_in(keys[3], 1), TOKENS // TOK_DEV)
    expert_ids_turns = jax.random.permutation(jax.random.fold_in(keys[3], 3), TOKENS // TOK_DEV)
    expert_ids = jax.vmap(lambda own, number: deal_out(jax.random.fold_in(keys[3], 2), own, number, TOK_DEV, EXPERTS, TOP, CAP, 2))(expert_ids_keys, expert_ids_turns).reshape((TOKENS, TOP))
    gate_weight = bell_draw(keys[4], (EXPERTS, D, H), D ** -0.5, 0.125, ((0, 32),))
    up_weight = bell_draw(keys[5], (EXPERTS, D, H), D ** -0.5, 0.125, ((0, 32),))
    down_weight = bell_draw(keys[6], (EXPERTS, D, H), H ** -0.5, 0.25, ((0, 32),))
    return {"tokens": tokens, "cotangent": cotangent, "gate_prob": gate_prob, "expert_ids": expert_ids, "gate_weight": gate_weight, "up_weight": up_weight, "down_weight": down_weight}


def slot_index(expert_col):
    hits = (expert_col[:, None] == jnp.arange(EXPERTS, dtype=jnp.int32)[None, :]).astype(jnp.int32)
    before = jnp.cumsum(hits, axis=0) - hits
    return (expert_col * CAP + jnp.sum(before * hits, axis=1)).astype(jnp.int32)


def place_rows(rows, where):
    buffer = jnp.zeros((EXPERTS * CAP,) + rows.shape[1:], rows.dtype)
    return buffer.at[where].set(rows)


def take_rows(rows, where):
    return rows[where]


def regroup(rows):
    shaped = rows.reshape((EXPERTS, EXPERTS, CAP) + rows.shape[2:])
    return jnp.swapaxes(shaped, 0, 1).reshape((EXPERTS, EXPERTS * CAP) + rows.shape[2:])


def expert_rows(x_rows, dy_rows, p_rows, w_gate, w_up, w_down):
    highest = lax.Precision.HIGHEST
    x_float = x_rows.astype(jnp.float32)
    gate_pre = jnp.einsum("erd,edh->erh", x_float, w_gate, precision=highest)
    up_pre = jnp.einsum("erd,edh->erh", x_float, w_up, precision=highest)
    sig_gate = jax.nn.sigmoid(gate_pre)
    active = gate_pre * sig_gate
    hidden = (active * up_pre).astype(jnp.bfloat16)
    hidden_float = hidden.astype(jnp.float32)
    restored = jnp.einsum("erh,edh->erd", hidden_float, w_down, precision=highest)
    dy_float = dy_rows.astype(jnp.float32)
    back_prob = jnp.sum(dy_float * restored, axis=-1).astype(jnp.bfloat16)
    scaled = (p_rows.astype(jnp.float32)[..., None] * dy_float).astype(jnp.bfloat16)
    scaled_float = scaled.astype(jnp.float32)
    back_hidden = jnp.einsum("erd,edh->erh", scaled_float, w_down, precision=highest)
    back_gate = (back_hidden * up_pre * sig_gate * (1.0 + gate_pre * (1.0 - sig_gate))).astype(jnp.bfloat16)
    back_up = (back_hidden * active).astype(jnp.bfloat16)
    gate_float = back_gate.astype(jnp.float32)
    up_float = back_up.astype(jnp.float32)
    back_rows = (jnp.einsum("erh,edh->erd", gate_float, w_gate, precision=highest)
                 + jnp.einsum("erh,edh->erd", up_float, w_up, precision=highest)).astype(jnp.bfloat16)
    part_gate = jnp.einsum("erd,erh->edh", x_float, gate_float, precision=highest)
    part_up = jnp.einsum("erd,erh->edh", x_float, up_float, precision=highest)
    part_down = jnp.einsum("erd,erh->edh", scaled_float, hidden_float, precision=highest)
    return back_rows, back_prob, part_gate, part_up, part_down


def rounded(part):
    return lax.optimization_barrier(part.astype(jnp.bfloat16)).astype(jnp.float32)


def reference(tokens, cotangent, gate_prob, expert_ids, gate_weight, up_weight, down_weight):
    group_total = TOKENS // (TOK_DEV * EXPERTS)
    x_all = tokens.reshape(group_total, EXPERTS, TOK_DEV, D)
    dy_all = cotangent.reshape(group_total, EXPERTS, TOK_DEV, D)
    p_all = gate_prob[:, 0].reshape(group_total, EXPERTS, TOK_DEV)
    ids_all = expert_ids[:, 0].reshape(group_total, EXPERTS, TOK_DEV).astype(jnp.int32)
    w_gate = gate_weight.astype(jnp.float32)
    w_up = up_weight.astype(jnp.float32)
    w_down = down_weight.astype(jnp.float32)

    def one_group(carry, items):
        x_grp, dy_grp, p_grp, id_grp = items
        target = jax.vmap(slot_index)(id_grp)
        x_buf = regroup(jax.vmap(place_rows)(x_grp, target))
        dy_buf = regroup(jax.vmap(place_rows)(dy_grp, target))
        p_buf = regroup(jax.vmap(place_rows)(p_grp, target))
        back_rows, back_prob, part_gate, part_up, part_down = expert_rows(x_buf, dy_buf, p_buf, w_gate, w_up, w_down)
        grad_rows = jax.vmap(take_rows)(regroup(back_rows), target)
        grad_probs = jax.vmap(take_rows)(regroup(back_prob), target)
        total_gate, total_up, total_down = carry
        carry = (total_gate + rounded(part_gate), total_up + rounded(part_up), total_down + rounded(part_down))
        return carry, (grad_rows, grad_probs)

    zeros = jnp.zeros((EXPERTS, D, H), jnp.float32)
    sums, outputs = lax.scan(one_group, (zeros, zeros, zeros), (x_all, dy_all, p_all, ids_all))
    grad_tokens = outputs[0].reshape(TOKENS, D)
    grad_prob = outputs[1].reshape(TOKENS, 1)
    return grad_tokens, grad_prob, sums[0], sums[1], sums[2]
```

```python
import functools

import jax
import jax.numpy as jnp
from jax import lax
from jax.experimental import pallas as pl
from jax.experimental.pallas import tpu as pltpu
from jax.sharding import PartitionSpec as P

MESH = pl.DeviceIdType.MESH
F32 = jnp.float32
BF16 = jnp.bfloat16
LANES = 128


def ring_steps(n, body):
    half = n // 2
    body(half)

    def pair(i, carry):
        body(half - i)
        body(half + i)
        return carry

    lax.fori_loop(1, half, pair, 0)


def iota(shape, dim):
    return lax.broadcasted_iota(jnp.int32, shape, dim).astype(F32)


def one_hot(mask):
    return jnp.where(mask, 1.0, 0.0)


def kernel(
    cap,
    n_ep,
    n_grp,
    x_ref,
    dy_ref,
    p_ref,
    ids_ref,
    ids_row_ref,
    wg_hbm,
    wu_hbm,
    wd_hbm,
    gt_ref,
    gp_ref,
    gg_ref,
    gu_ref,
    gd_ref,
    wg,
    wu,
    wd,
    wide,
    xs,
    ds,
    xr,
    dr,
    x2,
    d2,
    ys,
    yr,
    ps,
    pr,
    part,
    held,
    total,
    landed,
    w_sem,
    x_sems,
    d_sems,
    y_sems,
    p_sems,
    pair_sems,
    plane_sems,
):
    me = lax.axis_index("ep")
    grp = lax.axis_index("group")
    core = lax.rem(grp, 2)
    chip = grp // 2
    n_chip = n_grp // 2
    tok, width = x_ref.shape
    slots = n_ep * cap
    blocks = width // LANES
    rows = width // n_grp

    barrier = pltpu.get_barrier_semaphore()

    def greet_ring(k, carry):
        pl.semaphore_signal(
            barrier, inc=1, device_id={"ep": lax.rem(me + k, n_ep)}, device_id_type=MESH
        )
        return carry

    def greet_plane(k, carry):
        pl.semaphore_signal(
            barrier,
            inc=1,
            device_id={"group": lax.rem(chip + k, n_chip) * 2 + core},
            device_id_type=MESH,
        )
        return carry

    sibling = {"group": chip * 2 + 1 - core}
    lax.fori_loop(1, n_ep, greet_ring, 0)
    lax.fori_loop(1, n_chip, greet_plane, 0)
    pl.semaphore_signal(barrier, inc=1, device_id=sibling, device_id_type=MESH)

    weight_copies = [
        pltpu.make_async_copy(src.at[0], dst, w_sem.at[i])
        for i, (src, dst) in enumerate(((wg_hbm, wg), (wu_hbm, wu), (wd_hbm, wd)))
    ]
    for copy in weight_copies:
        copy.start()

    ids_col = ids_ref[...].astype(F32)
    ids_row = ids_row_ref[...].astype(F32)
    hits = one_hot(ids_col == iota((tok, n_ep), 1))
    earlier = one_hot(iota((tok, tok), 1) < iota((tok, tok), 0))
    before = jnp.dot(earlier.astype(BF16), hits.astype(BF16), preferred_element_type=F32)
    rank_col = jnp.sum(before * hits, axis=1, keepdims=True)
    target_col = ids_col * cap + rank_col
    hits_t = one_hot(ids_row == iota((n_ep, tok), 0))
    later = one_hot(iota((tok, tok), 0) < iota((tok, tok), 1))
    before_t = jnp.dot(hits_t.astype(BF16), later.astype(BF16), preferred_element_type=F32)
    rank_row = jnp.sum(before_t * hits_t, axis=0, keepdims=True)
    target_row = ids_row * cap + rank_row
    place = one_hot(target_row == iota((slots, tok), 0)).astype(BF16)
    take = one_hot(target_col == iota((tok, slots), 1)).astype(BF16)

    def spread(columns, block):
        wide[pl.ds(block, slots, stride=blocks), :] = columns

    def pack(dst):
        dst[...] = wide[...].reshape(slots, blocks, LANES).astype(BF16)

    def unpack(src):
        wide[...] = src[...].astype(F32).reshape(slots * blocks, LANES)

    def column(block):
        return wide[pl.ds(block, slots, stride=blocks), :].astype(BF16)

    def ring_copy(src, dst, sems, k, size):
        to = lax.rem(me + k, n_ep)
        return pltpu.make_async_remote_copy(
            src_ref=src.at[pl.ds(to * size, size)],
            dst_ref=dst.at[pl.ds(me * size, size)],
            send_sem=sems.at[0, k],
            recv_sem=sems.at[1, k],
            device_id={"ep": to},
            device_id_type=MESH,
        )

    def wait_ring(src, dst, sems, size):
        def one(k, carry):
            ring_copy(src, dst, sems, k, size).wait()
            return carry

        lax.fori_loop(1, n_ep, one, 0)

    step = 2 * LANES
    for j in range(width // step):
        placed = jnp.dot(place, x_ref[:, j * step : (j + 1) * step], preferred_element_type=F32)
        spread(placed[:, :LANES], 2 * j)
        spread(placed[:, LANES:], 2 * j + 1)
    pack(xs)
    xr[pl.ds(me * cap, cap)] = xs[pl.ds(me * cap, cap)]

    pl.semaphore_wait(barrier, n_ep - 1 + n_chip - 1 + 1)
    ring_steps(n_ep, lambda k: ring_copy(xs, xr, x_sems, k, cap).start())

    prob = p_ref[...].astype(F32)
    for j in range(width // step):
        scaled = (prob * dy_ref[:, j * step : (j + 1) * step].astype(F32)).astype(BF16)
        placed = jnp.dot(place, scaled, preferred_element_type=F32)
        spread(placed[:, :LANES], 2 * j)
        spread(placed[:, LANES:], 2 * j + 1)
    pack(ds)
    dr[pl.ds(me * cap, cap)] = ds[pl.ds(me * cap, cap)]
    ring_steps(n_ep, lambda k: ring_copy(ds, dr, d_sems, k, cap).start())

    for copy in weight_copies:
        copy.wait()
    wait_ring(xs, xr, x_sems, cap)
    unpack(xr)
    for b in range(blocks):
        x2[:, b * LANES : (b + 1) * LANES] = column(b)
    gate_pre = jnp.dot(x2[...], wg[...], preferred_element_type=F32)
    up_pre = jnp.dot(x2[...], wu[...], preferred_element_type=F32)
    sig = jax.nn.sigmoid(gate_pre)
    active = gate_pre * sig
    hidden = (active * up_pre).astype(BF16)
    gate_slope = up_pre * sig * (1.0 + gate_pre * (1.0 - sig))

    wait_ring(ds, dr, d_sems, cap)
    unpack(dr)
    for b in range(blocks):
        d2[:, b * LANES : (b + 1) * LANES] = column(b)
    back_hidden = jnp.dot(d2[...], wd[...], preferred_element_type=F32)
    back_gate = (back_hidden * gate_slope).astype(BF16)
    back_up = (back_hidden * active).astype(BF16)
    contract_h = (((1,), (1,)), ((), ()))
    for j in range(width // step):
        span = slice(j * step, (j + 1) * step)
        back = lax.dot_general(back_gate, wg[span, :], contract_h, preferred_element_type=F32)
        back += lax.dot_general(back_up, wu[span, :], contract_h, preferred_element_type=F32)
        spread(back[:, :LANES], 2 * j)
        spread(back[:, LANES:], 2 * j + 1)
    pack(ys)
    yr[pl.ds(me * cap, cap)] = ys[pl.ds(me * cap, cap)]
    ring_steps(n_ep, lambda k: ring_copy(ys, yr, y_sems, k, cap).start())

    weighted = jnp.sum(hidden.astype(F32) * back_hidden, axis=1, keepdims=True)
    slot_of = iota((slots, LANES), 0)
    lane = iota((slots, LANES), 1)
    source = jnp.floor((slot_of + 0.5) * (1.0 / cap))
    by_lane = weighted * one_hot(slot_of - source * cap == lane)
    row_iota = iota((n_ep, slots), 0)
    offset = iota((n_ep, slots), 1) - row_iota * cap
    collect = one_hot((offset >= 0.0) & (offset < cap))
    prob_rows = jnp.dot(
        collect, by_lane, precision=lax.Precision.HIGHEST, preferred_element_type=F32
    )
    ps[...] = prob_rows.reshape(n_ep, 1, LANES)
    pr[pl.ds(me, 1)] = ps[pl.ds(me, 1)]
    ring_steps(n_ep, lambda k: ring_copy(ps, pr, p_sems, k, 1).start())

    contract_rows = (((0,), (0,)), ((), ()))

    def pair_copy(c):
        return pltpu.make_async_remote_copy(
            src_ref=part.at[1 - core, c],
            dst_ref=held.at[c],
            send_sem=pair_sems.at[0, c],
            recv_sem=pair_sems.at[1, c],
            device_id=sibling,
            device_id_type=MESH,
        )

    def plane_copy(k):
        to = lax.rem(chip + k, n_chip)
        return pltpu.make_async_remote_copy(
            src_ref=total.at[to],
            dst_ref=landed.at[chip],
            send_sem=plane_sems.at[0, k],
            recv_sem=plane_sems.at[1, k],
            device_id={"group": to * 2 + core},
            device_id_type=MESH,
        )

    def partials(k, carry):
        c = lax.rem(chip + k, n_chip)
        span = pl.ds(pl.multiple_of(c * 2 * rows, 2 * rows), 2 * rows)
        for m, (left, right) in enumerate(((x2, back_gate), (x2, back_up), (d2, hidden))):
            term = lax.dot_general(left[:, span], right, contract_rows, preferred_element_type=F32)
            part[0, c, m] = term[:rows].astype(BF16)
            part[1, c, m] = term[rows:].astype(BF16)
        pair_copy(c).start()
        return carry

    lax.fori_loop(1, n_chip + 1, partials, 0)

    def add_pair(c):
        pair_copy(c).wait()
        total[c] = (part[core, c].astype(F32) + held[c].astype(F32)).astype(BF16)

    def pair_sums(k, carry):
        add_pair(lax.rem(chip + k, n_chip))
        plane_copy(k).start()
        return carry

    lax.fori_loop(1, n_chip, pair_sums, 0)
    add_pair(chip)

    def wait_plane(k, carry):
        plane_copy(k).wait()
        return carry

    landed[pl.ds(chip, 1)] = total[pl.ds(chip, 1)]
    lax.fori_loop(1, n_chip, wait_plane, 0)
    for m, out in enumerate((gg_ref, gu_ref, gd_ref)):
        acc = landed[0, m].astype(F32)
        for c in range(1, n_chip):
            acc += landed[c, m].astype(F32)
        out[0] = acc

    wait_ring(ps, pr, p_sems, 1)
    table = pr[...].reshape(n_ep, LANES)
    mine = jnp.dot(hits, table, precision=lax.Precision.HIGHEST, preferred_element_type=F32)
    picked = jnp.sum(
        mine * one_hot(rank_col == iota((tok, LANES), 1)), axis=1, keepdims=True
    )
    gp_ref[...] = (picked / prob).astype(BF16)

    wait_ring(ys, yr, y_sems, cap)
    unpack(yr)
    for b in range(blocks):
        gt_ref[:, b * LANES : (b + 1) * LANES] = jnp.dot(
            take, column(b), preferred_element_type=F32
        ).astype(BF16)


def per_device(tokens, cotangent, gate_prob, expert_ids, gate_weight, up_weight, down_weight):
    n_ep = lax.axis_size("ep")
    n_grp = lax.axis_size("group")
    tok, width = tokens.shape
    hid = gate_weight.shape[-1]
    cap = tok // n_ep + max(1, tok // (4 * n_ep))
    slots = n_ep * cap
    blocks = width // LANES
    rows = width // n_grp
    n_chip = n_grp // 2
    vmem = pl.BlockSpec(memory_space=pltpu.VMEM)
    hbm = pl.BlockSpec(memory_space=pl.ANY)
    tiled = pltpu.VMEM((slots, blocks, LANES), BF16)
    flat = pltpu.VMEM((slots, width), BF16)
    probs = pltpu.VMEM((n_ep, 1, LANES), F32)
    slices = pltpu.VMEM((n_chip, 3, rows, hid), BF16)
    ring_sems = pltpu.SemaphoreType.DMA((2, n_ep))
    plane_sems = pltpu.SemaphoreType.DMA((2, n_chip))
    grad = jax.ShapeDtypeStruct((1, rows, hid), F32)
    return pl.pallas_call(
        functools.partial(kernel, cap, n_ep, n_grp),
        out_shape=(
            jax.ShapeDtypeStruct((tok, width), BF16),
            jax.ShapeDtypeStruct((tok, 1), BF16),
            grad,
            grad,
            grad,
        ),
        in_specs=[vmem] * 5 + [hbm] * 3,
        out_specs=[vmem] * 5,
        scratch_shapes=[
            pltpu.VMEM((width, hid), BF16),
            pltpu.VMEM((width, hid), BF16),
            pltpu.VMEM((width, hid), BF16),
            pltpu.VMEM((slots * blocks, LANES), F32),
            tiled,
            tiled,
            tiled,
            tiled,
            flat,
            flat,
            tiled,
            tiled,
            probs,
            probs,
            pltpu.VMEM((2, n_chip, 3, rows, hid), BF16),
            slices,
            slices,
            slices,
            pltpu.SemaphoreType.DMA((3,)),
            ring_sems,
            ring_sems,
            ring_sems,
            ring_sems,
            plane_sems,
            plane_sems,
        ],
        compiler_params=pltpu.CompilerParams(
            collective_id=0, has_side_effects=True, vmem_limit_bytes=56 << 20
        ),
    )(
        tokens,
        cotangent,
        gate_prob,
        expert_ids,
        expert_ids.reshape(1, tok),
        gate_weight,
        up_weight,
        down_weight,
    )


def solution(mesh):
    in_specs = (
        P(("group", "ep"), None),
        P(("group", "ep"), None),
        P(("group", "ep"), None),
        P(("group", "ep"), None),
        P("ep", None, None),
        P("ep", None, None),
        P("ep", None, None),
    )
    out_specs = (
        P(("group", "ep"), None),
        P(("group", "ep"), None),
        P("ep", "group", None),
        P("ep", "group", None),
        P("ep", "group", None),
    )
    return jax.shard_map(
        per_device, mesh=mesh, in_specs=in_specs, out_specs=out_specs, check_vma=False
    )
```

```python
import functools
import math

import jax
import jax.numpy as jnp
from jax import lax
from jax.experimental import pallas as pl
from jax.experimental.pallas import tpu as pltpu
from jax.sharding import PartitionSpec as P

MESH = pl.DeviceIdType.MESH
F32 = jnp.float32
BF16 = jnp.bfloat16
LANES = 128


def batch_steps(n, batch, body):
    half, quarter = n // 2, n // 4
    body(half if batch == 0 else quarter)

    def pair(i, carry):
        near = quarter - i
        body(half - i if batch == 0 else near)
        body(half + i if batch == 0 else n - near)
        return carry

    lax.fori_loop(1, quarter, pair, 0)
    if batch == 0:
        body(3 * quarter)


def iota(shape, dim):
    return lax.broadcasted_iota(jnp.int32, shape, dim).astype(F32)


def one_hot(mask):
    return jnp.where(mask, 1.0, 0.0)


def kernel(
    cap,
    n_ep,
    side,
    x_ref,
    dy_ref,
    p_ref,
    ids_ref,
    wg_hbm,
    wu_hbm,
    wd_hbm,
    gt_ref,
    gp_ref,
    gg_ref,
    gu_ref,
    gd_ref,
    wg,
    wu,
    wd,
    wide,
    scaled,
    xs,
    ds,
    xr,
    dr,
    x2,
    d2,
    bg,
    bu,
    ys,
    yr,
    ps,
    pr,
    part,
    held,
    mid,
    mid_in,
    last,
    last_in,
    w_sem,
    x_sems,
    d_sems,
    y_sems,
    p_sems,
    pair_sems,
    mid_sems,
    last_sems,
):
    me = lax.axis_index("ep")
    grp = lax.axis_index("group")
    core = lax.rem(grp, 2)
    chip = grp // 2
    n_chip = side * side
    at_y, at_x = chip // side, lax.rem(chip, side)
    tok, width = x_ref.shape
    slots = n_ep * cap
    blocks = width // LANES
    rows = width // (2 * n_chip)
    quarter = n_ep // 4
    some = slots // 2

    def on_plane(half, a, b):
        return {"group": ((b * side + a) if half == 0 else (a * side + b)) * 2 + core}

    own_a, own_b = (at_x, at_y), (at_y, at_x)
    sibling = {"group": chip * 2 + 1 - core}
    barrier = pltpu.get_barrier_semaphore()

    def greet(device):
        pl.semaphore_signal(barrier, inc=1, device_id=device, device_id_type=MESH)

    def greet_ring(k, carry):
        greet({"ep": lax.rem(me + k, n_ep)})
        return carry

    lax.fori_loop(1, n_ep, greet_ring, 0)
    for half in range(2):
        for k in range(1, side):
            greet(on_plane(half, lax.rem(own_a[half] + k, side), own_b[half]))
    greet(sibling)

    weight_copies = [
        pltpu.make_async_copy(src.at[0], dst, w_sem.at[i])
        for i, (src, dst) in enumerate(((wg_hbm, wg), (wu_hbm, wu), (wd_hbm, wd)))
    ]
    for copy in weight_copies:
        copy.start()

    turned = lax.rem(ids_ref[...] + (2 * n_ep - quarter - 1) - me, n_ep).astype(F32)
    hits_t = one_hot(turned == iota((n_ep, tok), 0))
    later = one_hot(iota((tok, tok), 0) < iota((tok, tok), 1))
    before_t = jnp.dot(hits_t.astype(BF16), later.astype(BF16), preferred_element_type=F32)
    rank_row = jnp.sum(before_t * hits_t, axis=0, keepdims=True)
    target_row = turned * cap + rank_row
    place = one_hot(target_row == iota((slots, tok), 0)).astype(BF16)
    diagonal = iota((tok, tok), 0) == iota((tok, tok), 1)

    def upright(row):
        return jnp.sum(jnp.where(diagonal, row, 0.0), axis=1, keepdims=True)

    step = 2 * LANES

    def spread(batch, columns, block):
        wide[pl.ds(batch * some * blocks + block, some, stride=blocks), :] = columns

    def tiles(batch):
        return slice(batch * some * blocks, (batch + 1) * some * blocks)

    def pack(batch, dst):
        dst[batch * some : (batch + 1) * some] = (
            wide[tiles(batch), :].reshape(some, blocks, LANES).astype(BF16)
        )

    def unpack(batch, src, dst):
        wide[tiles(batch), :] = (
            src[batch * some : (batch + 1) * some].astype(F32).reshape(some * blocks, LANES)
        )
        for b in range(blocks):
            dst[batch * some : (batch + 1) * some, b * LANES : (b + 1) * LANES] = wide[
                pl.ds(batch * some * blocks + b, some, stride=blocks), :
            ].astype(BF16)

    def sent_at(k):
        return lax.rem(k + n_ep - quarter - 1, n_ep)

    def got_at(k):
        return lax.rem(2 * n_ep - k - quarter, n_ep)

    def out_copy(src, dst, sems, k, size):
        return pltpu.make_async_remote_copy(
            src_ref=src.at[pl.ds(sent_at(k) * size, size)],
            dst_ref=dst.at[pl.ds(got_at(k) * size, size)],
            send_sem=sems.at[0, k],
            recv_sem=sems.at[1, k],
            device_id={"ep": lax.rem(me + k, n_ep)},
            device_id_type=MESH,
        )

    def home_copy(src, dst, sems, k, size):
        return pltpu.make_async_remote_copy(
            src_ref=src.at[pl.ds(got_at(k) * size, size)],
            dst_ref=dst.at[pl.ds(sent_at(k) * size, size)],
            send_sem=sems.at[0, k],
            recv_sem=sems.at[1, k],
            device_id={"ep": lax.rem(me + n_ep - k, n_ep)},
            device_id_type=MESH,
        )

    own_sent, own_got = n_ep - quarter - 1, n_ep - quarter

    def to_slots(batch, values, dst):
        chosen = place[batch * some : (batch + 1) * some]
        for j in range(width // step):
            span = slice(j * step, (j + 1) * step)
            placed = jnp.dot(chosen, values[:, span], preferred_element_type=F32)
            spread(batch, placed[:, :LANES], 2 * j)
            spread(batch, placed[:, LANES:], 2 * j + 1)
        pack(batch, dst)

    to_slots(0, x_ref, xs)
    pl.semaphore_wait(barrier, n_ep - 1 + 2 * (side - 1) + 1)
    batch_steps(n_ep, 0, lambda k: out_copy(xs, xr, x_sems, k, cap).start())
    to_slots(1, x_ref, xs)
    batch_steps(n_ep, 1, lambda k: out_copy(xs, xr, x_sems, k, cap).start())
    xr[own_got * cap : (own_got + 1) * cap] = xs[own_sent * cap : (own_sent + 1) * cap]

    prob_row = p_ref[...].astype(F32)
    prob = upright(prob_row)
    scaled[...] = (prob * dy_ref[...].astype(F32)).astype(BF16)
    for batch in range(2):
        to_slots(batch, scaled, ds)
        batch_steps(n_ep, batch, lambda k: out_copy(ds, dr, d_sems, k, cap).start())
    dr[own_got * cap : (own_got + 1) * cap] = ds[own_sent * cap : (own_sent + 1) * cap]

    for copy in weight_copies:
        copy.wait()
    for batch in range(2):
        batch_steps(n_ep, batch, lambda k: out_copy(xs, xr, x_sems, k, cap).wait())
        unpack(batch, xr, x2)
    gate_pre = jnp.dot(x2[...], wg[...], preferred_element_type=F32)
    up_pre = jnp.dot(x2[...], wu[...], preferred_element_type=F32)
    sig = jax.nn.sigmoid(gate_pre)
    active = gate_pre * sig
    hidden = (active * up_pre).astype(BF16)
    gate_slope = up_pre * sig * (1.0 + gate_pre * (1.0 - sig))

    slot_of = iota((some, LANES), 0)
    slot_lane = slot_of - jnp.floor((slot_of + 0.5) * (1.0 / cap)) * cap == iota((some, LANES), 1)
    offset = iota((n_ep // 2, some), 1) - iota((n_ep // 2, some), 0) * cap
    collect = one_hot((offset >= 0.0) & (offset < cap))
    contract_h = (((1,), (1,)), ((), ()))
    for batch in range(2):
        own = slice(batch * some, (batch + 1) * some)
        batch_steps(n_ep, batch, lambda k: out_copy(ds, dr, d_sems, k, cap).wait())
        unpack(batch, dr, d2)
        back_hidden = jnp.dot(d2[own, :], wd[...], preferred_element_type=F32)
        back_gate = (back_hidden * gate_slope[own]).astype(BF16)
        back_up = (back_hidden * active[own]).astype(BF16)
        bg[own, :] = back_gate
        bu[own, :] = back_up
        for j in range(width // step):
            span = slice(j * step, (j + 1) * step)
            back = lax.dot_general(back_gate, wg[span, :], contract_h, preferred_element_type=F32)
            back += lax.dot_general(back_up, wu[span, :], contract_h, preferred_element_type=F32)
            spread(batch, back[:, :LANES], 2 * j)
            spread(batch, back[:, LANES:], 2 * j + 1)
        pack(batch, ys)
        batch_steps(n_ep, batch, lambda k: home_copy(ys, yr, y_sems, k, cap).start())
        weighted = jnp.sum(hidden[own].astype(F32) * back_hidden, axis=1, keepdims=True)
        prob_rows = jnp.dot(
            collect,
            weighted * one_hot(slot_lane),
            precision=lax.Precision.HIGHEST,
            preferred_element_type=F32,
        )
        ps[batch * (n_ep // 2) : (batch + 1) * (n_ep // 2)] = prob_rows.reshape(
            n_ep // 2, 1, LANES
        )
    yr[own_sent * cap : (own_sent + 1) * cap] = ys[own_got * cap : (own_got + 1) * cap]
    pr[own_sent : own_sent + 1] = ps[own_got : own_got + 1]
    for batch in range(2):
        batch_steps(n_ep, batch, lambda k: home_copy(ps, pr, p_sems, k, 1).start())

    contract_rows = (((0,), (0,)), ((), ()))
    few = rows // 2

    def pair_copy(half, a, b):
        return pltpu.make_async_remote_copy(
            src_ref=part.at[1 - core, half, a, b],
            dst_ref=held.at[half, a, b],
            send_sem=pair_sems.at[0, half, a * side + b],
            recv_sem=pair_sems.at[1, half, a * side + b],
            device_id=sibling,
            device_id_type=MESH,
        )

    def partials(k, carry):
        c = lax.rem(chip + k, n_chip)
        c_y, c_x = c // side, lax.rem(c, side)
        span = pl.ds(pl.multiple_of(c * 2 * rows, 2 * rows), 2 * rows)
        for m, (left, right) in enumerate(((x2, bg[...]), (x2, bu[...]), (d2, hidden))):
            term = lax.dot_general(
                left[:, span], right, contract_rows, preferred_element_type=F32
            ).astype(BF16)
            for i in range(2):
                part[i, 0, c_x, c_y, m] = term[i * rows : i * rows + few]
                part[i, 1, c_y, c_x, m] = term[i * rows + few : (i + 1) * rows]
        pair_copy(0, c_x, c_y).start()
        pair_copy(1, c_y, c_x).start()
        return carry

    lax.fori_loop(1, n_chip + 1, partials, 0)

    def mid_copy(half, k):
        a = lax.rem(own_a[half] + k, side)
        return pltpu.make_async_remote_copy(
            src_ref=mid.at[half, a],
            dst_ref=mid_in.at[half, k],
            send_sem=mid_sems.at[0, half, k],
            recv_sem=mid_sems.at[1, half, k],
            device_id=on_plane(half, a, own_b[half]),
            device_id_type=MESH,
        )

    def last_copy(half, k):
        b = lax.rem(own_b[half] + k, side)
        return pltpu.make_async_remote_copy(
            src_ref=last.at[half, b],
            dst_ref=last_in.at[half, k],
            send_sem=last_sems.at[0, half, k],
            recv_sem=last_sems.at[1, half, k],
            device_id=on_plane(half, own_a[half], b),
            device_id_type=MESH,
        )

    for k in list(range(1, side)) + [0]:
        for half in range(2):
            a = lax.rem(own_a[half] + k, side)

            def add_pair(b, carry):
                pair_copy(half, a, b).wait()
                mid[half, a, b] = (
                    part[core, half, a, b].astype(F32) + held[half, a, b].astype(F32)
                ).astype(BF16)
                return carry

            lax.fori_loop(0, side, add_pair, 0)
            if k:
                mid_copy(half, k).start()

    for half in range(2):
        for k in range(1, side):
            mid_copy(half, k).wait()

        def add_mid(k, carry):
            b = lax.rem(own_b[half] + k, side)
            acc = mid[half, own_a[half], b].astype(F32)
            for i in range(1, side):
                acc += mid_in[half, i, b].astype(F32)
            last[half, b] = acc.astype(BF16)
            return carry

        lax.fori_loop(1, side + 1, add_mid, 0)
        for k in range(1, side):
            last_copy(half, k).start()

    for half in range(2):
        for k in range(1, side):
            last_copy(half, k).wait()
        for m, out in enumerate((gg_ref, gu_ref, gd_ref)):
            acc = last[half, own_b[half], m].astype(F32)
            for i in range(1, side):
                acc += last_in[half, i, m].astype(F32)
            out[0, half * few : (half + 1) * few] = acc

    hits = one_hot(upright(turned) == iota((tok, n_ep), 1))
    take = one_hot(upright(target_row) == iota((tok, slots), 1)).astype(BF16)
    lanes = one_hot(upright(rank_row) == iota((tok, LANES), 1))
    batch_steps(n_ep, 0, lambda k: home_copy(ys, yr, y_sems, k, cap).wait())
    unpack(0, yr, d2)
    for j in range(width // step):
        span = slice(j * step, (j + 1) * step)
        gt_ref[:, span] = jnp.dot(
            take[:, :some], d2[:some, span], preferred_element_type=F32
        ).astype(BF16)
    for batch in range(2):
        batch_steps(n_ep, batch, lambda k: home_copy(ps, pr, p_sems, k, 1).wait())
    table = pr[...].reshape(n_ep, LANES)
    mine = jnp.dot(hits, table, precision=lax.Precision.HIGHEST, preferred_element_type=F32)
    picked = jnp.sum(mine * lanes, axis=1, keepdims=True)
    grad_prob = jnp.sum(jnp.where(diagonal, picked, 0.0), axis=0, keepdims=True) / prob_row
    gp_ref[...] = grad_prob.astype(BF16)
    batch_steps(n_ep, 1, lambda k: home_copy(ys, yr, y_sems, k, cap).wait())
    unpack(1, yr, d2)
    for j in range(width // step):
        span = slice(j * step, (j + 1) * step)
        near = jnp.dot(take[:, some:], d2[some:, span], preferred_element_type=F32)
        gt_ref[:, span] = (gt_ref[:, span].astype(F32) + near).astype(BF16)


def hand_on(*refs):
    count = len(refs) // 2
    for src, dst in zip(refs[:count], refs[count:]):
        dst[...] = src[...]


def per_device(tokens, cotangent, gate_prob, expert_ids, gate_weight, up_weight, down_weight):
    n_ep = lax.axis_size("ep")
    n_grp = lax.axis_size("group")
    tok, width = tokens.shape
    hid = gate_weight.shape[-1]
    cap = tok // n_ep + max(1, tok // (4 * n_ep))
    slots = n_ep * cap
    blocks = width // LANES
    rows = width // n_grp
    side = math.isqrt(n_grp // 2)
    vmem = pl.BlockSpec(memory_space=pltpu.VMEM)
    hbm = pl.BlockSpec(memory_space=pl.ANY)
    weight = pltpu.VMEM((width, hid), BF16)
    tiled = pltpu.VMEM((slots, blocks, LANES), BF16)
    flat = pltpu.VMEM((slots, width), BF16)
    narrow = pltpu.VMEM((slots, hid), BF16)
    probs = pltpu.VMEM((n_ep, 1, LANES), F32)
    slices = (side, 3, rows // 2, hid)
    squares = pltpu.VMEM((2, side) + slices, BF16)
    ring_sems = pltpu.SemaphoreType.DMA((2, n_ep))
    side_sems = pltpu.SemaphoreType.DMA((2, 2, side))
    grad = jax.ShapeDtypeStruct((1, rows, hid), F32)
    shapes = (
        jax.ShapeDtypeStruct((tok, width), BF16),
        jax.ShapeDtypeStruct((1, tok), BF16),
        grad,
        grad,
        grad,
    )
    results = pl.pallas_call(
        functools.partial(kernel, cap, n_ep, side),
        out_shape=shapes,
        in_specs=[vmem] * 4 + [hbm] * 3,
        out_specs=[vmem] * 5,
        scratch_shapes=[
            weight,
            weight,
            weight,
            pltpu.VMEM((slots * blocks, LANES), F32),
            pltpu.VMEM((tok, width), BF16),
            tiled,
            tiled,
            tiled,
            tiled,
            flat,
            flat,
            narrow,
            narrow,
            tiled,
            tiled,
            probs,
            probs,
            pltpu.VMEM((2, 2, side) + slices, BF16),
            squares,
            squares,
            squares,
            pltpu.VMEM((2,) + slices, BF16),
            pltpu.VMEM((2,) + slices, BF16),
            pltpu.SemaphoreType.DMA((3,)),
            ring_sems,
            ring_sems,
            ring_sems,
            ring_sems,
            pltpu.SemaphoreType.DMA((2, 2, side * side)),
            side_sems,
            side_sems,
        ],
        compiler_params=pltpu.CompilerParams(
            collective_id=0, has_side_effects=True, vmem_limit_bytes=56 << 20
        ),
    )(
        tokens,
        cotangent,
        gate_prob.reshape(1, tok),
        expert_ids.reshape(1, tok),
        gate_weight,
        up_weight,
        down_weight,
    )
    results = pl.pallas_call(
        hand_on,
        out_shape=shapes,
        in_specs=[vmem] * 5,
        out_specs=[vmem] * 5,
    )(*results)
    return (results[0], results[1].reshape(tok, 1)) + tuple(results[2:])


def solution(mesh):
    in_specs = (
        P(("group", "ep"), None),
        P(("group", "ep"), None),
        P(("group", "ep"), None),
        P(("group", "ep"), None),
        P("ep", None, None),
        P("ep", None, None),
        P("ep", None, None),
    )
    out_specs = (
        P(("group", "ep"), None),
        P(("group", "ep"), None),
        P("ep", "group", None),
        P("ep", "group", None),
        P("ep", "group", None),
    )
    return jax.shard_map(
        per_device, mesh=mesh, in_specs=in_specs, out_specs=out_specs, check_vma=False
    )
```

```python
import functools
import math

import jax
import jax.numpy as jnp
from jax import lax
from jax.experimental import pallas as pl
from jax.experimental.pallas import tpu as pltpu
from jax.sharding import PartitionSpec as P

MESH = pl.DeviceIdType.MESH
F32 = jnp.float32
BF16 = jnp.bfloat16
LANES = 128


def batch_steps(n, batch, body):
    half, quarter = n // 2, n // 4
    body(half if batch == 0 else quarter)

    def pair(i, carry):
        near = quarter - i
        body(half - i if batch == 0 else near)
        body(half + i if batch == 0 else n - near)
        return carry

    lax.fori_loop(1, quarter, pair, 0)
    if batch == 0:
        body(3 * quarter)


def iota(shape, dim):
    return lax.broadcasted_iota(jnp.int32, shape, dim).astype(F32)


def one_hot(mask):
    return jnp.where(mask, 1.0, 0.0)


def kernel(
    cap,
    n_ep,
    side,
    x_ref,
    dy_ref,
    p_ref,
    ids_ref,
    wg_hbm,
    wu_hbm,
    wd_hbm,
    gt_ref,
    gp_ref,
    gg_ref,
    gu_ref,
    gd_ref,
    wg,
    wu,
    wd,
    wide,
    scaled,
    xs,
    ds,
    xr,
    dr,
    x2,
    d2,
    bg,
    bu,
    ys,
    yr,
    ps,
    pr,
    part,
    held,
    mid,
    mid_in,
    last,
    last_in,
    w_sem,
    x_sems,
    d_sems,
    y_sems,
    p_sems,
    pair_sems,
    mid_sems,
    last_sems,
    ready,
):
    me = lax.axis_index("ep")
    grp = lax.axis_index("group")
    core = lax.rem(grp, 2)
    chip = grp // 2
    n_chip = side * side
    at_y, at_x = chip // side, lax.rem(chip, side)
    tok, width = x_ref.shape
    slots = n_ep * cap
    blocks = width // LANES
    rows = width // (2 * n_chip)
    quarter = n_ep // 4
    some = slots // 2

    def on_plane(half, a, b):
        return {"group": ((b * side + a) if half == 0 else (a * side + b)) * 2 + core}

    own_a, own_b = (at_x, at_y), (at_y, at_x)
    sibling = {"group": chip * 2 + 1 - core}
    barrier = pltpu.get_barrier_semaphore()

    def greet(device):
        pl.semaphore_signal(barrier, inc=1, device_id=device, device_id_type=MESH)

    for k in (1, n_ep - 1):
        greet({"ep": lax.rem(me + k, n_ep)})
    for half in range(2):
        for k in range(1, side):
            greet(on_plane(half, lax.rem(own_a[half] + k, side), own_b[half]))
    greet(sibling)
    pl.semaphore_wait(barrier, 2 + 2 * (side - 1) + 1)

    weight_copies = [
        pltpu.make_async_copy(src.at[0], dst, w_sem.at[i])
        for i, (src, dst) in enumerate(((wg_hbm, wg), (wu_hbm, wu), (wd_hbm, wd)))
    ]
    for copy in weight_copies:
        copy.start()

    def tell(level):
        for way, k in enumerate((1 << level, n_ep - (1 << level))):
            pl.semaphore_signal(
                ready.at[level, way],
                inc=1,
                device_id={"ep": lax.rem(me + k, n_ep)},
                device_id_type=MESH,
            )

    tell(0)

    turned = lax.rem(ids_ref[...] + (2 * n_ep - quarter - 1) - me, n_ep).astype(F32)
    hits_t = one_hot(turned == iota((n_ep, tok), 0))
    later = one_hot(iota((tok, tok), 0) < iota((tok, tok), 1))
    before_t = jnp.dot(hits_t.astype(BF16), later.astype(BF16), preferred_element_type=F32)
    rank_row = jnp.sum(before_t * hits_t, axis=0, keepdims=True)
    target_row = turned * cap + rank_row
    place = one_hot(target_row == iota((slots, tok), 0)).astype(BF16)
    diagonal = iota((tok, tok), 0) == iota((tok, tok), 1)

    def upright(row):
        return jnp.sum(jnp.where(diagonal, row, 0.0), axis=1, keepdims=True)

    step = 2 * LANES

    def spread(batch, columns, block):
        wide[pl.ds(batch * some * blocks + block, some, stride=blocks), :] = columns

    def tiles(batch):
        return slice(batch * some * blocks, (batch + 1) * some * blocks)

    def pack(batch, dst):
        dst[batch * some : (batch + 1) * some] = (
            wide[tiles(batch), :].reshape(some, blocks, LANES).astype(BF16)
        )

    def unpack(batch, src, dst):
        wide[tiles(batch), :] = (
            src[batch * some : (batch + 1) * some].astype(F32).reshape(some * blocks, LANES)
        )
        for b in range(blocks):
            dst[batch * some : (batch + 1) * some, b * LANES : (b + 1) * LANES] = wide[
                pl.ds(batch * some * blocks + b, some, stride=blocks), :
            ].astype(BF16)

    def sent_at(k):
        return lax.rem(k + n_ep - quarter - 1, n_ep)

    def got_at(k):
        return lax.rem(2 * n_ep - k - quarter, n_ep)

    def out_copy(src, dst, sems, k, size):
        return pltpu.make_async_remote_copy(
            src_ref=src.at[pl.ds(sent_at(k) * size, size)],
            dst_ref=dst.at[pl.ds(got_at(k) * size, size)],
            send_sem=sems.at[0, k],
            recv_sem=sems.at[1, k],
            device_id={"ep": lax.rem(me + k, n_ep)},
            device_id_type=MESH,
        )

    def home_copy(src, dst, sems, k, size):
        return pltpu.make_async_remote_copy(
            src_ref=src.at[pl.ds(got_at(k) * size, size)],
            dst_ref=dst.at[pl.ds(sent_at(k) * size, size)],
            send_sem=sems.at[0, k],
            recv_sem=sems.at[1, k],
            device_id={"ep": lax.rem(me + n_ep - k, n_ep)},
            device_id_type=MESH,
        )

    own_sent, own_got = n_ep - quarter - 1, n_ep - quarter

    def to_slots(batch, values, dst):
        chosen = place[batch * some : (batch + 1) * some]
        for j in range(width // step):
            span = slice(j * step, (j + 1) * step)
            placed = jnp.dot(chosen, values[:, span], preferred_element_type=F32)
            spread(batch, placed[:, :LANES], 2 * j)
            spread(batch, placed[:, LANES:], 2 * j + 1)
        pack(batch, dst)

    def send_near(k):
        out_copy(xs, xr, x_sems, k, cap).start()
        if k < quarter:
            out_copy(xs, xr, x_sems, n_ep - k, cap).start()

    to_slots(1, x_ref, xs)
    send_near(1)
    levels = (n_ep // 2).bit_length() - 1
    for level in range(levels):
        for way in range(2):
            pl.semaphore_wait(ready.at[level, way], 1)
        if level < levels - 1:
            tell(level + 1)
            for k in range((1 << level) + 1, (2 << level) + 1):
                send_near(k)
        if level == 0:
            to_slots(0, x_ref, xs)
    batch_steps(n_ep, 0, lambda k: out_copy(xs, xr, x_sems, k, cap).start())
    xr[own_got * cap : (own_got + 1) * cap] = xs[own_sent * cap : (own_sent + 1) * cap]

    prob_row = p_ref[...].astype(F32)
    prob = upright(prob_row)
    scaled[...] = (prob * dy_ref[...].astype(F32)).astype(BF16)
    for batch in range(2):
        to_slots(batch, scaled, ds)
        batch_steps(n_ep, batch, lambda k: out_copy(ds, dr, d_sems, k, cap).start())
    dr[own_got * cap : (own_got + 1) * cap] = ds[own_sent * cap : (own_sent + 1) * cap]

    for copy in weight_copies:
        copy.wait()
    for batch in range(2):
        batch_steps(n_ep, batch, lambda k: out_copy(xs, xr, x_sems, k, cap).wait())
        unpack(batch, xr, x2)
    gate_pre = jnp.dot(x2[...], wg[...], preferred_element_type=F32)
    up_pre = jnp.dot(x2[...], wu[...], preferred_element_type=F32)
    sig = jax.nn.sigmoid(gate_pre)
    active = gate_pre * sig
    hidden = (active * up_pre).astype(BF16)
    gate_slope = up_pre * sig * (1.0 + gate_pre * (1.0 - sig))

    slot_of = iota((some, LANES), 0)
    slot_lane = slot_of - jnp.floor((slot_of + 0.5) * (1.0 / cap)) * cap == iota((some, LANES), 1)
    offset = iota((n_ep // 2, some), 1) - iota((n_ep // 2, some), 0) * cap
    collect = one_hot((offset >= 0.0) & (offset < cap))
    contract_h = (((1,), (1,)), ((), ()))
    for batch in range(2):
        own = slice(batch * some, (batch + 1) * some)
        batch_steps(n_ep, batch, lambda k: out_copy(ds, dr, d_sems, k, cap).wait())
        unpack(batch, dr, d2)
        back_hidden = jnp.dot(d2[own, :], wd[...], preferred_element_type=F32)
        back_gate = (back_hidden * gate_slope[own]).astype(BF16)
        back_up = (back_hidden * active[own]).astype(BF16)
        bg[own, :] = back_gate
        bu[own, :] = back_up
        for j in range(width // step):
            span = slice(j * step, (j + 1) * step)
            back = lax.dot_general(back_gate, wg[span, :], contract_h, preferred_element_type=F32)
            back += lax.dot_general(back_up, wu[span, :], contract_h, preferred_element_type=F32)
            spread(batch, back[:, :LANES], 2 * j)
            spread(batch, back[:, LANES:], 2 * j + 1)
        pack(batch, ys)
        batch_steps(n_ep, batch, lambda k: home_copy(ys, yr, y_sems, k, cap).start())
        weighted = jnp.sum(hidden[own].astype(F32) * back_hidden, axis=1, keepdims=True)
        prob_rows = jnp.dot(
            collect,
            weighted * one_hot(slot_lane),
            precision=lax.Precision.HIGHEST,
            preferred_element_type=F32,
        )
        ps[batch * (n_ep // 2) : (batch + 1) * (n_ep // 2)] = prob_rows.reshape(
            n_ep // 2, 1, LANES
        )
        batch_steps(n_ep, batch, lambda k: home_copy(ps, pr, p_sems, k, 1).start())
    yr[own_sent * cap : (own_sent + 1) * cap] = ys[own_got * cap : (own_got + 1) * cap]
    pr[own_sent : own_sent + 1] = ps[own_got : own_got + 1]

    contract_rows = (((0,), (0,)), ((), ()))
    few = rows // 2

    def pair_copy(half, a, b):
        return pltpu.make_async_remote_copy(
            src_ref=part.at[1 - core, half, a, b],
            dst_ref=held.at[half, a, b],
            send_sem=pair_sems.at[0, half, a * side + b],
            recv_sem=pair_sems.at[1, half, a * side + b],
            device_id=sibling,
            device_id_type=MESH,
        )

    def partials(k, carry):
        c = lax.rem(chip + k, n_chip)
        c_y, c_x = c // side, lax.rem(c, side)
        span = pl.ds(pl.multiple_of(c * 2 * rows, 2 * rows), 2 * rows)
        for m, (left, right) in enumerate(((x2, bg[...]), (x2, bu[...]), (d2, hidden))):
            term = lax.dot_general(
                left[:, span], right, contract_rows, preferred_element_type=F32
            ).astype(BF16)
            for i in range(2):
                part[i, 0, c_x, c_y, m] = term[i * rows : i * rows + few]
                part[i, 1, c_y, c_x, m] = term[i * rows + few : (i + 1) * rows]
        pair_copy(0, c_x, c_y).start()
        pair_copy(1, c_y, c_x).start()
        return carry

    lax.fori_loop(1, n_chip + 1, partials, 0)

    def mid_copy(half, k):
        a = lax.rem(own_a[half] + k, side)
        return pltpu.make_async_remote_copy(
            src_ref=mid.at[half, a],
            dst_ref=mid_in.at[half, k],
            send_sem=mid_sems.at[0, half, k],
            recv_sem=mid_sems.at[1, half, k],
            device_id=on_plane(half, a, own_b[half]),
            device_id_type=MESH,
        )

    def last_copy(half, k):
        b = lax.rem(own_b[half] + k, side)
        return pltpu.make_async_remote_copy(
            src_ref=last.at[half, b],
            dst_ref=last_in.at[half, k],
            send_sem=last_sems.at[0, half, k],
            recv_sem=last_sems.at[1, half, k],
            device_id=on_plane(half, own_a[half], b),
            device_id_type=MESH,
        )

    for k in list(range(1, side)) + [0]:
        for half in range(2):
            a = lax.rem(own_a[half] + k, side)

            def add_pair(b, carry):
                pair_copy(half, a, b).wait()
                mid[half, a, b] = (
                    part[core, half, a, b].astype(F32) + held[half, a, b].astype(F32)
                ).astype(BF16)
                return carry

            lax.fori_loop(0, side, add_pair, 0)
            if k:
                mid_copy(half, k).start()

    for half in range(2):
        for k in range(1, side):
            mid_copy(half, k).wait()

        def add_mid(k, carry):
            b = lax.rem(own_b[half] + k, side)
            acc = mid[half, own_a[half], b].astype(F32)
            for i in range(1, side):
                acc += mid_in[half, i, b].astype(F32)
            last[half, b] = acc.astype(BF16)
            return carry

        lax.fori_loop(1, side + 1, add_mid, 0)
        for k in range(1, side):
            last_copy(half, k).start()

    for half in range(2):
        for k in range(1, side):
            last_copy(half, k).wait()
        for m, out in enumerate((gg_ref, gu_ref, gd_ref)):
            acc = last[half, own_b[half], m].astype(F32)
            for i in range(1, side):
                acc += last_in[half, i, m].astype(F32)
            out[0, half * few : (half + 1) * few] = acc

    hits = one_hot(upright(turned) == iota((tok, n_ep), 1))
    take = one_hot(upright(target_row) == iota((tok, slots), 1)).astype(BF16)
    lanes = one_hot(upright(rank_row) == iota((tok, LANES), 1))
    batch_steps(n_ep, 0, lambda k: home_copy(ys, yr, y_sems, k, cap).wait())
    unpack(0, yr, d2)
    for j in range(width // step):
        span = slice(j * step, (j + 1) * step)
        gt_ref[:, span] = jnp.dot(
            take[:, :some], d2[:some, span], preferred_element_type=F32
        ).astype(BF16)
    for batch in range(2):
        batch_steps(n_ep, batch, lambda k: home_copy(ps, pr, p_sems, k, 1).wait())
    table = pr[...].reshape(n_ep, LANES)
    mine = jnp.dot(hits, table, precision=lax.Precision.HIGHEST, preferred_element_type=F32)
    picked = jnp.sum(mine * lanes, axis=1, keepdims=True)
    grad_prob = jnp.sum(jnp.where(diagonal, picked, 0.0), axis=0, keepdims=True) / prob_row
    gp_ref[...] = grad_prob.astype(BF16)
    batch_steps(n_ep, 1, lambda k: home_copy(ys, yr, y_sems, k, cap).wait())
    unpack(1, yr, d2)
    for j in range(width // step):
        span = slice(j * step, (j + 1) * step)
        near = jnp.dot(take[:, some:], d2[some:, span], preferred_element_type=F32)
        gt_ref[:, span] = (gt_ref[:, span].astype(F32) + near).astype(BF16)


def hand_on(*refs):
    count = len(refs) // 2
    for src, dst in zip(refs[:count], refs[count:]):
        dst[...] = src[...]


def per_device(tokens, cotangent, gate_prob, expert_ids, gate_weight, up_weight, down_weight):
    n_ep = lax.axis_size("ep")
    n_grp = lax.axis_size("group")
    tok, width = tokens.shape
    hid = gate_weight.shape[-1]
    cap = tok // n_ep + max(1, tok // (4 * n_ep))
    slots = n_ep * cap
    blocks = width // LANES
    rows = width // n_grp
    side = math.isqrt(n_grp // 2)
    vmem = pl.BlockSpec(memory_space=pltpu.VMEM)
    hbm = pl.BlockSpec(memory_space=pl.ANY)
    weight = pltpu.VMEM((width, hid), BF16)
    tiled = pltpu.VMEM((slots, blocks, LANES), BF16)
    flat = pltpu.VMEM((slots, width), BF16)
    narrow = pltpu.VMEM((slots, hid), BF16)
    probs = pltpu.VMEM((n_ep, 1, LANES), F32)
    slices = (side, 3, rows // 2, hid)
    squares = pltpu.VMEM((2, side) + slices, BF16)
    ring_sems = pltpu.SemaphoreType.DMA((2, n_ep))
    side_sems = pltpu.SemaphoreType.DMA((2, 2, side))
    grad = jax.ShapeDtypeStruct((1, rows, hid), F32)
    shapes = (
        jax.ShapeDtypeStruct((tok, width), BF16),
        jax.ShapeDtypeStruct((1, tok), BF16),
        grad,
        grad,
        grad,
    )
    results = pl.pallas_call(
        functools.partial(kernel, cap, n_ep, side),
        out_shape=shapes,
        in_specs=[vmem] * 4 + [hbm] * 3,
        out_specs=[vmem] * 5,
        scratch_shapes=[
            weight,
            weight,
            weight,
            pltpu.VMEM((slots * blocks, LANES), F32),
            pltpu.VMEM((tok, width), BF16),
            tiled,
            tiled,
            tiled,
            tiled,
            flat,
            flat,
            narrow,
            narrow,
            tiled,
            tiled,
            probs,
            probs,
            pltpu.VMEM((2, 2, side) + slices, BF16),
            squares,
            squares,
            squares,
            pltpu.VMEM((2,) + slices, BF16),
            pltpu.VMEM((2,) + slices, BF16),
            pltpu.SemaphoreType.DMA((3,)),
            ring_sems,
            ring_sems,
            ring_sems,
            ring_sems,
            pltpu.SemaphoreType.DMA((2, 2, side * side)),
            side_sems,
            side_sems,
            pltpu.SemaphoreType.REGULAR(((n_ep // 2).bit_length() - 1, 2)),
        ],
        compiler_params=pltpu.CompilerParams(
            collective_id=0, has_side_effects=True, vmem_limit_bytes=56 << 20
        ),
    )(
        tokens,
        cotangent,
        gate_prob.reshape(1, tok),
        expert_ids.reshape(1, tok),
        gate_weight,
        up_weight,
        down_weight,
    )
    results = pl.pallas_call(
        hand_on,
        out_shape=shapes,
        in_specs=[vmem] * 5,
        out_specs=[vmem] * 5,
    )(*results)
    return (results[0], results[1].reshape(tok, 1)) + tuple(results[2:])


def solution(mesh):
    in_specs = (
        P(("group", "ep"), None),
        P(("group", "ep"), None),
        P(("group", "ep"), None),
        P(("group", "ep"), None),
        P("ep", None, None),
        P("ep", None, None),
        P("ep", None, None),
    )
    out_specs = (
        P(("group", "ep"), None),
        P(("group", "ep"), None),
        P("ep", "group", None),
        P("ep", "group", None),
        P("ep", "group", None),
    )
    return jax.shard_map(
        per_device, mesh=mesh, in_specs=in_specs, out_specs=out_specs, check_vma=False
    )
```

```python
import functools
import math

import jax
import jax.numpy as jnp
from jax import lax
from jax.experimental import pallas as pl
from jax.experimental.pallas import tpu as pltpu
from jax.sharding import PartitionSpec as P

MESH = pl.DeviceIdType.MESH
F32 = jnp.float32
BF16 = jnp.bfloat16
LANES = 128


def batch_steps(n, batch, body):
    half, quarter = n // 2, n // 4
    body(half if batch == 0 else quarter)

    def pair(i, carry):
        near = quarter - i
        body(half - i if batch == 0 else near)
        body(half + i if batch == 0 else n - near)
        return carry

    lax.fori_loop(1, quarter, pair, 0)
    if batch == 0:
        body(3 * quarter)


def iota(shape, dim):
    return lax.broadcasted_iota(jnp.int32, shape, dim).astype(F32)


def one_hot(mask):
    return jnp.where(mask, 1.0, 0.0)


def kernel(
    cap,
    n_ep,
    side,
    x_hbm,
    dy_hbm,
    p_ref,
    ids_ref,
    wg_hbm,
    wu_hbm,
    wd_hbm,
    gt_ref,
    gp_ref,
    gg_ref,
    gu_ref,
    gd_ref,
    x_ref,
    dy_ref,
    wg,
    wu,
    wd,
    wide,
    scaled,
    xs,
    ds,
    xr,
    dr,
    x2,
    d2,
    bg,
    bu,
    ys,
    yr,
    ps,
    pr,
    part,
    held,
    mid,
    mid_in,
    last,
    last_in,
    row_sem,
    w_sem,
    x_sems,
    d_sems,
    y_sems,
    p_sems,
    pair_sems,
    mid_sems,
    last_sems,
    ready,
):
    me = lax.axis_index("ep")
    grp = lax.axis_index("group")
    core = lax.rem(grp, 2)
    chip = grp // 2
    n_chip = side * side
    at_y, at_x = chip // side, lax.rem(chip, side)
    tok, width = x_ref.shape
    row_copies = [
        pltpu.make_async_copy(x_hbm, x_ref, row_sem.at[0]),
        pltpu.make_async_copy(dy_hbm, dy_ref, row_sem.at[1]),
    ]
    slots = n_ep * cap
    blocks = width // LANES
    rows = width // (2 * n_chip)
    quarter = n_ep // 4
    some = slots // 2

    def on_plane(half, a, b):
        return {"group": ((b * side + a) if half == 0 else (a * side + b)) * 2 + core}

    own_a, own_b = (at_x, at_y), (at_y, at_x)
    sibling = {"group": chip * 2 + 1 - core}
    barrier = pltpu.get_barrier_semaphore()

    def greet(device):
        pl.semaphore_signal(barrier, inc=1, device_id=device, device_id_type=MESH)

    for k in (1, n_ep - 1):
        greet({"ep": lax.rem(me + k, n_ep)})
    for half in range(2):
        for k in range(1, side):
            greet(on_plane(half, lax.rem(own_a[half] + k, side), own_b[half]))
    greet(sibling)
    for copy in row_copies:
        copy.start()
    pl.semaphore_wait(barrier, 2 + 2 * (side - 1) + 1)

    def tell(level):
        for way, k in enumerate((1 << level, n_ep - (1 << level))):
            pl.semaphore_signal(
                ready.at[level, way],
                inc=1,
                device_id={"ep": lax.rem(me + k, n_ep)},
                device_id_type=MESH,
            )

    tell(0)
    weight_copies = [
        pltpu.make_async_copy(src.at[0], dst, w_sem.at[i])
        for i, (src, dst) in enumerate(((wg_hbm, wg), (wu_hbm, wu), (wd_hbm, wd)))
    ]
    for copy in weight_copies:
        copy.start()

    turned = lax.rem(ids_ref[...] + (2 * n_ep - quarter - 1) - me, n_ep).astype(F32)
    hits_t = one_hot(turned == iota((n_ep, tok), 0))
    later = one_hot(iota((tok, tok), 0) < iota((tok, tok), 1))
    before_t = jnp.dot(hits_t.astype(BF16), later.astype(BF16), preferred_element_type=F32)
    rank_row = jnp.sum(before_t * hits_t, axis=0, keepdims=True)
    target_row = turned * cap + rank_row
    place = one_hot(target_row == iota((slots, tok), 0)).astype(BF16)
    diagonal = iota((tok, tok), 0) == iota((tok, tok), 1)

    def upright(row):
        return jnp.sum(jnp.where(diagonal, row, 0.0), axis=1, keepdims=True)

    step = 2 * LANES

    def spread(batch, columns, block):
        wide[pl.ds(batch * some * blocks + block, some, stride=blocks), :] = columns

    def tiles(batch):
        return slice(batch * some * blocks, (batch + 1) * some * blocks)

    def pack(batch, dst):
        dst[batch * some : (batch + 1) * some] = (
            wide[tiles(batch), :].reshape(some, blocks, LANES).astype(BF16)
        )

    def unpack(batch, src, dst):
        wide[tiles(batch), :] = (
            src[batch * some : (batch + 1) * some].astype(F32).reshape(some * blocks, LANES)
        )
        for b in range(blocks):
            dst[batch * some : (batch + 1) * some, b * LANES : (b + 1) * LANES] = wide[
                pl.ds(batch * some * blocks + b, some, stride=blocks), :
            ].astype(BF16)

    def sent_at(k):
        return lax.rem(k + n_ep - quarter - 1, n_ep)

    def got_at(k):
        return lax.rem(2 * n_ep - k - quarter, n_ep)

    def out_copy(src, dst, sems, k, size):
        return pltpu.make_async_remote_copy(
            src_ref=src.at[pl.ds(sent_at(k) * size, size)],
            dst_ref=dst.at[pl.ds(got_at(k) * size, size)],
            send_sem=sems.at[0, k],
            recv_sem=sems.at[1, k],
            device_id={"ep": lax.rem(me + k, n_ep)},
            device_id_type=MESH,
        )

    def home_copy(src, dst, sems, k, size):
        return pltpu.make_async_remote_copy(
            src_ref=src.at[pl.ds(got_at(k) * size, size)],
            dst_ref=dst.at[pl.ds(sent_at(k) * size, size)],
            send_sem=sems.at[0, k],
            recv_sem=sems.at[1, k],
            device_id={"ep": lax.rem(me + n_ep - k, n_ep)},
            device_id_type=MESH,
        )

    own_sent, own_got = n_ep - quarter - 1, n_ep - quarter

    def to_slots(batch, values, dst):
        chosen = place[batch * some : (batch + 1) * some]
        for j in range(width // step):
            span = slice(j * step, (j + 1) * step)
            placed = jnp.dot(chosen, values[:, span], preferred_element_type=F32)
            spread(batch, placed[:, :LANES], 2 * j)
            spread(batch, placed[:, LANES:], 2 * j + 1)
        pack(batch, dst)

    def send_near(k):
        out_copy(xs, xr, x_sems, k, cap).start()
        if k < quarter:
            out_copy(xs, xr, x_sems, n_ep - k, cap).start()

    levels = (n_ep // 2).bit_length() - 1
    for level in range(levels):
        for way in range(2):
            pl.semaphore_wait(ready.at[level, way], 1)
        if level < levels - 1:
            tell(level + 1)
        if level == 0:
            row_copies[0].wait()
            to_slots(1, x_ref, xs)
            send_near(1)
        if level < levels - 1:
            for k in range((1 << level) + 1, (2 << level) + 1):
                send_near(k)
        if level == max(levels - 2, 0):
            to_slots(0, x_ref, xs)
    batch_steps(n_ep, 0, lambda k: out_copy(xs, xr, x_sems, k, cap).start())
    xr[own_got * cap : (own_got + 1) * cap] = xs[own_sent * cap : (own_sent + 1) * cap]

    row_copies[1].wait()
    prob_row = p_ref[...].astype(F32)
    prob = upright(prob_row)
    scaled[...] = (prob * dy_ref[...].astype(F32)).astype(BF16)
    for batch in range(2):
        to_slots(batch, scaled, ds)
        batch_steps(n_ep, batch, lambda k: out_copy(ds, dr, d_sems, k, cap).start())
    dr[own_got * cap : (own_got + 1) * cap] = ds[own_sent * cap : (own_sent + 1) * cap]

    for copy in weight_copies:
        copy.wait()
    for batch in range(2):
        batch_steps(n_ep, batch, lambda k: out_copy(xs, xr, x_sems, k, cap).wait())
        unpack(batch, xr, x2)
    gate_pre = jnp.dot(x2[...], wg[...], preferred_element_type=F32)
    up_pre = jnp.dot(x2[...], wu[...], preferred_element_type=F32)
    sig = jax.nn.sigmoid(gate_pre)
    active = gate_pre * sig
    hidden = (active * up_pre).astype(BF16)
    gate_slope = up_pre * sig * (1.0 + gate_pre * (1.0 - sig))

    slot_of = iota((some, LANES), 0)
    slot_lane = slot_of - jnp.floor((slot_of + 0.5) * (1.0 / cap)) * cap == iota((some, LANES), 1)
    offset = iota((n_ep // 2, some), 1) - iota((n_ep // 2, some), 0) * cap
    collect = one_hot((offset >= 0.0) & (offset < cap))
    contract_h = (((1,), (1,)), ((), ()))
    for batch in range(2):
        own = slice(batch * some, (batch + 1) * some)
        batch_steps(n_ep, batch, lambda k: out_copy(ds, dr, d_sems, k, cap).wait())
        unpack(batch, dr, d2)
        back_hidden = jnp.dot(d2[own, :], wd[...], preferred_element_type=F32)
        back_gate = (back_hidden * gate_slope[own]).astype(BF16)
        back_up = (back_hidden * active[own]).astype(BF16)
        bg[own, :] = back_gate
        bu[own, :] = back_up
        for j in range(width // step):
            span = slice(j * step, (j + 1) * step)
            back = lax.dot_general(back_gate, wg[span, :], contract_h, preferred_element_type=F32)
            back += lax.dot_general(back_up, wu[span, :], contract_h, preferred_element_type=F32)
            spread(batch, back[:, :LANES], 2 * j)
            spread(batch, back[:, LANES:], 2 * j + 1)
        pack(batch, ys)
        batch_steps(n_ep, batch, lambda k: home_copy(ys, yr, y_sems, k, cap).start())
        weighted = jnp.sum(hidden[own].astype(F32) * back_hidden, axis=1, keepdims=True)
        prob_rows = jnp.dot(
            collect,
            weighted * one_hot(slot_lane),
            precision=lax.Precision.HIGHEST,
            preferred_element_type=F32,
        )
        ps[batch * (n_ep // 2) : (batch + 1) * (n_ep // 2)] = prob_rows.reshape(
            n_ep // 2, 1, LANES
        )
        batch_steps(n_ep, batch, lambda k: home_copy(ps, pr, p_sems, k, 1).start())
    yr[own_sent * cap : (own_sent + 1) * cap] = ys[own_got * cap : (own_got + 1) * cap]
    pr[own_sent : own_sent + 1] = ps[own_got : own_got + 1]

    contract_rows = (((0,), (0,)), ((), ()))
    few = rows // 2

    def pair_copy(half, a, b):
        return pltpu.make_async_remote_copy(
            src_ref=part.at[1 - core, half, a, b],
            dst_ref=held.at[half, a, b],
            send_sem=pair_sems.at[0, half, a * side + b],
            recv_sem=pair_sems.at[1, half, a * side + b],
            device_id=sibling,
            device_id_type=MESH,
        )

    def partials(k, carry):
        c = lax.rem(chip + k, n_chip)
        c_y, c_x = c // side, lax.rem(c, side)
        span = pl.ds(pl.multiple_of(c * 2 * rows, 2 * rows), 2 * rows)
        for m, (left, right) in enumerate(((x2, bg[...]), (x2, bu[...]), (d2, hidden))):
            term = lax.dot_general(
                left[:, span], right, contract_rows, preferred_element_type=F32
            ).astype(BF16)
            for i in range(2):
                part[i, 0, c_x, c_y, m] = term[i * rows : i * rows + few]
                part[i, 1, c_y, c_x, m] = term[i * rows + few : (i + 1) * rows]
        pair_copy(0, c_x, c_y).start()
        pair_copy(1, c_y, c_x).start()
        return carry

    lax.fori_loop(1, n_chip + 1, partials, 0)

    def mid_copy(half, k):
        a = lax.rem(own_a[half] + k, side)
        return pltpu.make_async_remote_copy(
            src_ref=mid.at[half, a],
            dst_ref=mid_in.at[half, k],
            send_sem=mid_sems.at[0, half, k],
            recv_sem=mid_sems.at[1, half, k],
            device_id=on_plane(half, a, own_b[half]),
            device_id_type=MESH,
        )

    def last_copy(half, k):
        b = lax.rem(own_b[half] + k, side)
        return pltpu.make_async_remote_copy(
            src_ref=last.at[half, b],
            dst_ref=last_in.at[half, k],
            send_sem=last_sems.at[0, half, k],
            recv_sem=last_sems.at[1, half, k],
            device_id=on_plane(half, own_a[half], b),
            device_id_type=MESH,
        )

    for k in list(range(1, side)) + [0]:
        for half in range(2):
            a = lax.rem(own_a[half] + k, side)

            def add_pair(b, carry):
                pair_copy(half, a, b).wait()
                mid[half, a, b] = (
                    part[core, half, a, b].astype(F32) + held[half, a, b].astype(F32)
                ).astype(BF16)
                return carry

            lax.fori_loop(0, side, add_pair, 0)
            if k:
                mid_copy(half, k).start()

    for half in range(2):
        for k in range(1, side):
            mid_copy(half, k).wait()

        def add_mid(k, carry):
            b = lax.rem(own_b[half] + k, side)
            acc = mid[half, own_a[half], b].astype(F32)
            for i in range(1, side):
                acc += mid_in[half, i, b].astype(F32)
            last[half, b] = acc.astype(BF16)
            return carry

        lax.fori_loop(1, side + 1, add_mid, 0)
        for k in range(1, side):
            last_copy(half, k).start()

    for half in range(2):
        for k in range(1, side):
            last_copy(half, k).wait()
        for m, out in enumerate((gg_ref, gu_ref, gd_ref)):
            acc = last[half, own_b[half], m].astype(F32)
            for i in range(1, side):
                acc += last_in[half, i, m].astype(F32)
            out[0, half * few : (half + 1) * few] = acc

    hits = one_hot(upright(turned) == iota((tok, n_ep), 1))
    take = one_hot(upright(target_row) == iota((tok, slots), 1)).astype(BF16)
    lanes = one_hot(upright(rank_row) == iota((tok, LANES), 1))
    batch_steps(n_ep, 0, lambda k: home_copy(ys, yr, y_sems, k, cap).wait())
    unpack(0, yr, d2)
    for j in range(width // step):
        span = slice(j * step, (j + 1) * step)
        gt_ref[:, span] = jnp.dot(
            take[:, :some], d2[:some, span], preferred_element_type=F32
        ).astype(BF16)
    for batch in range(2):
        batch_steps(n_ep, batch, lambda k: home_copy(ps, pr, p_sems, k, 1).wait())
    table = pr[...].reshape(n_ep, LANES)
    mine = jnp.dot(hits, table, precision=lax.Precision.HIGHEST, preferred_element_type=F32)
    picked = jnp.sum(mine * lanes, axis=1, keepdims=True)
    grad_prob = jnp.sum(jnp.where(diagonal, picked, 0.0), axis=0, keepdims=True) / prob_row
    gp_ref[...] = grad_prob.astype(BF16)
    batch_steps(n_ep, 1, lambda k: home_copy(ys, yr, y_sems, k, cap).wait())
    unpack(1, yr, d2)
    for j in range(width // step):
        span = slice(j * step, (j + 1) * step)
        near = jnp.dot(take[:, some:], d2[some:, span], preferred_element_type=F32)
        gt_ref[:, span] = (gt_ref[:, span].astype(F32) + near).astype(BF16)


def hand_on(*refs):
    count = len(refs) // 2
    for src, dst in zip(refs[:count], refs[count:]):
        dst[...] = src[...]


def per_device(tokens, cotangent, gate_prob, expert_ids, gate_weight, up_weight, down_weight):
    n_ep = lax.axis_size("ep")
    n_grp = lax.axis_size("group")
    tok, width = tokens.shape
    hid = gate_weight.shape[-1]
    cap = tok // n_ep + max(1, tok // (4 * n_ep))
    slots = n_ep * cap
    blocks = width // LANES
    rows = width // n_grp
    side = math.isqrt(n_grp // 2)
    vmem = pl.BlockSpec(memory_space=pltpu.VMEM)
    hbm = pl.BlockSpec(memory_space=pl.ANY)
    weight = pltpu.VMEM((width, hid), BF16)
    tiled = pltpu.VMEM((slots, blocks, LANES), BF16)
    flat = pltpu.VMEM((slots, width), BF16)
    narrow = pltpu.VMEM((slots, hid), BF16)
    probs = pltpu.VMEM((n_ep, 1, LANES), F32)
    slices = (side, 3, rows // 2, hid)
    squares = pltpu.VMEM((2, side) + slices, BF16)
    ring_sems = pltpu.SemaphoreType.DMA((2, n_ep))
    side_sems = pltpu.SemaphoreType.DMA((2, 2, side))
    grad = jax.ShapeDtypeStruct((1, rows, hid), F32)
    shapes = (
        jax.ShapeDtypeStruct((tok, width), BF16),
        jax.ShapeDtypeStruct((1, tok), BF16),
        grad,
        grad,
        grad,
    )
    results = pl.pallas_call(
        functools.partial(kernel, cap, n_ep, side),
        out_shape=shapes,
        in_specs=[hbm] * 2 + [vmem] * 2 + [hbm] * 3,
        out_specs=[vmem] * 5,
        scratch_shapes=[
            pltpu.VMEM((tok, width), BF16),
            pltpu.VMEM((tok, width), BF16),
            weight,
            weight,
            weight,
            pltpu.VMEM((slots * blocks, LANES), F32),
            pltpu.VMEM((tok, width), BF16),
            tiled,
            tiled,
            tiled,
            tiled,
            flat,
            flat,
            narrow,
            narrow,
            tiled,
            tiled,
            probs,
            probs,
            pltpu.VMEM((2, 2, side) + slices, BF16),
            squares,
            squares,
            squares,
            pltpu.VMEM((2,) + slices, BF16),
            pltpu.VMEM((2,) + slices, BF16),
            pltpu.SemaphoreType.DMA((2,)),
            pltpu.SemaphoreType.DMA((3,)),
            ring_sems,
            ring_sems,
            ring_sems,
            ring_sems,
            pltpu.SemaphoreType.DMA((2, 2, side * side)),
            side_sems,
            side_sems,
            pltpu.SemaphoreType.REGULAR(((n_ep // 2).bit_length() - 1, 2)),
        ],
        compiler_params=pltpu.CompilerParams(
            collective_id=0, has_side_effects=True, vmem_limit_bytes=56 << 20
        ),
    )(
        tokens,
        cotangent,
        gate_prob.reshape(1, tok),
        expert_ids.reshape(1, tok),
        gate_weight,
        up_weight,
        down_weight,
    )
    results = pl.pallas_call(
        hand_on,
        out_shape=shapes,
        in_specs=[vmem] * 5,
        out_specs=[vmem] * 5,
    )(*results)
    return (results[0], results[1].reshape(tok, 1)) + tuple(results[2:])


def solution(mesh):
    in_specs = (
        P(("group", "ep"), None),
        P(("group", "ep"), None),
        P(("group", "ep"), None),
        P(("group", "ep"), None),
        P("ep", None, None),
        P("ep", None, None),
        P("ep", None, None),
    )
    out_specs = (
        P(("group", "ep"), None),
        P(("group", "ep"), None),
        P("ep", "group", None),
        P("ep", "group", None),
        P("ep", "group", None),
    )
    return jax.shard_map(
        per_device, mesh=mesh, in_specs=in_specs, out_specs=out_specs, check_vma=False
    )
```
